32 devices in a mesh: dp: 8 (over z, y), mp: 4 (over x, core).
Axes of the slice: x: 2, y: 2, z: 4, core: 2. Of those that a mesh axis runs over, the one named last changes fastest.
Arguments:
- tokens: bfloat16 [16384, 896], P(('dp', 'mp')), may hold values from -6 to 6
- cotangent: bfloat16 [16384, 896], P(('dp', 'mp')), may hold values from -6 to 6
- segments: int32 [8, 2048], P('dp'), may hold values from 0 to 7, never falling along the last dimension, each value on 1 to 1537 neighbouring positions
- qkv_weight: float32 [896, 1152], P('dp'), may hold values from -0.1875 to 0.1875
- qkv_moment: float32 [896, 1152], P('dp'), may hold values from -128 to 128
- qkv_square: float32 [896, 1152], P('dp'), may hold values from 32.768 to 131.072
- qkv_bias: float32 [1152], P('dp'), may hold values from -3 to 3
- bias_moment: float32 [1152], P('dp'), may hold values from -2560 to 2560
- bias_square: float32 [1152], P('dp'), may hold values from 14680.064 to 58720.258
- out_weight: float32 [896, 896], P('dp'), may hold values from -1.5 to 1.5
- out_moment: float32 [896, 896], P('dp'), may hold values from -6 to 6
- out_square: float32 [896, 896], P('dp'), may hold values from 0.24576 to 0.98304
- gate_up_weight: float32 [896, 2, 4864], P('dp', None, 'mp'), may hold values from -0.1875 to 0.1875
- gate_up_moment: float32 [896, 2, 4864], P('dp', None, 'mp'), may hold values from -40 to 40
- gate_up_square: float32 [896, 2, 4864], P('dp', None, 'mp'), may hold values from 3.2768 to 13.1072
- down_weight: float32 [4864, 896], P('mp', 'dp'), may hold values from -0.15625 to 0.15625
- down_moment: float32 [4864, 896], P('mp', 'dp'), may hold values from -48 to 48
- down_square: float32 [4864, 896], P('mp', 'dp'), may hold values from 5.89824 to 23.59296
- norm_gains: float32 [2, 896], P(None, 'dp'), may hold values from 0.5 to 1.5
- gains_moment: float32 [2, 896], P(None, 'dp'), may hold values from -128 to 128
- gains_square: float32 [2, 896], P(None, 'dp'), may hold values from 40.96 to 163.84
Outputs:
- layer_out: bfloat16 [16384, 896], P(('dp', 'mp'))
- input_grad: bfloat16 [16384, 896], P(('dp', 'mp'))
- qkv_grad: float32 [896, 1152], P('dp')
- qkv_moment_new: float32 [896, 1152], P('dp')
- qkv_square_new: float32 [896, 1152], P('dp')
- qkv_weight_new: float32 [896, 1152], P('dp')
- bias_grad: float32 [1152], P('dp')
- bias_moment_new: float32 [1152], P('dp')
- bias_square_new: float32 [1152], P('dp')
- bias_new: float32 [1152], P('dp')
- out_grad: float32 [896, 896], P('dp')
- out_moment_new: float32 [896, 896], P('dp')
- out_square_new: float32 [896, 896], P('dp')
- out_weight_new: float32 [896, 896], P('dp')
- gate_up_grad: float32 [896, 2, 4864], P('dp', None, 'mp')
- gate_up_moment_new: float32 [896, 2, 4864], P('dp', None, 'mp')
- gate_up_square_new: float32 [896, 2, 4864], P('dp', None, 'mp')
- gate_up_weight_new: float32 [896, 2, 4864], P('dp', None, 'mp')
- down_grad: float32 [4864, 896], P('mp', 'dp')
- down_moment_new: float32 [4864, 896], P('mp', 'dp')
- down_square_new: float32 [4864, 896], P('mp', 'dp')
- down_weight_new: float32 [4864, 896], P('mp', 'dp')
- gains_grad: float32 [2, 896], P(None, 'dp')
- gains_moment_new: float32 [2, 896], P(None, 'dp')
- gains_square_new: float32 [2, 896], P(None, 'dp')
- gains_new: float32 [2, 896], P(None, 'dp')
The draws below stay inside these ranges and needn't reach their ends.
Inputs may be any that keep to these rules, and one draw needn't show every extreme that they name: `segments`: document numbers never fall along a sequence and start at 0; each document has 1 to 1537 tokens and one of each sequence has exactly 1537.
All inputs are finite; a program needn't handle non-finite values.
Results may differ from the reference program's by a relative error of at most 0.02.
Values may be sent and summed in bfloat16 or wider, within the bound.
A program may use at most 256 MiB of HBM per device.

```python
import math
import jax
import jax.numpy as jnp
import numpy as np
from jax import lax

D = 896
QUERY_HEADS = 14
KEY_VALUE_HEADS = 2
HEAD_SIZE = 64
FF = 4864
STEP = 10
QUERY_WIDTH = 896
QKV = 1152
SEQ = 2048
NSEQ = 8
TOKENS = 16384
DOCS = 8
LONGEST = 1537


def raised(drawn, rng, source, target, blocks, factor):
    owner, partner = [(jnp.arange(drawn.shape[dim]) // (drawn.shape[dim] // blocks)).reshape([-1 if axis == dim else 1 for axis in range(drawn.ndim)]) for dim in (source, target)]
    chosen = jax.random.permutation(rng, blocks)[partner]
    strong = (owner == chosen) | (owner == (partner + blocks // 2) % blocks)
    return jnp.where(strong, factor * drawn, drawn)


def level_of(key, dims, shards, smallest, top_value):
    factor_of = 1.0
    for dim, parts in shards:
        heights = jax.random.uniform(jax.random.fold_in(jax.random.fold_in(key, 6), dim), (parts,), jnp.float32, smallest / len(shards), top_value / len(shards))
        factor_of = factor_of * jnp.repeat(jnp.exp(heights), dims[dim] // parts).reshape((-1,) + (1,) * (len(dims) - 1 - dim))
    return factor_of


def profile(count, total, reach, slope):
    loads = [(1 << 20) // math.isqrt(grade ** slope) + 1 for grade in range(2, count + 1)]
    rest, counts = total - reach - (count - 1), [1] * (count - 1)
    while rest > 0:
        movable = [i for i in range(count - 1) if counts[i] < reach]
        whole, left = sum([loads[i] for i in movable]), rest
        for i in movable:
            addition = min(reach - counts[i], max(1, left * loads[i] // whole), rest)
            counts[i] = counts[i] + addition
            rest = rest - addition
    return np.array([reach] + counts)


def uneven(key, number_of, total, bound, slope):
    if number_of == 2:
        one = jax.random.randint(key, (), max(1, total - bound), min(bound, total - 1) + 1)
        return jnp.stack([one, total - one])
    tallies = jnp.asarray(profile(number_of, total, bound, slope), jnp.int32)
    twos = (number_of - 1) // 2
    source_of, receiver = tallies[1:1 + 2 * twos:2], tallies[2:2 + 2 * twos:2]
    slack = jnp.minimum(source_of - 1, bound - receiver)
    passed = jax.random.randint(jax.random.fold_in(key, 1), (twos,), 0, 1 << 20) % (slack + 1)
    tallies = tallies.at[1:1 + 2 * twos:2].set(source_of - passed).at[2:2 + 2 * twos:2].set(receiver + passed)
    return tallies[jax.random.permutation(jax.random.fold_in(key, 2), number_of)]


def bell_draw(key, dims, deviation, reach, cuts=(), held_as=jnp.bfloat16):
    drawn = deviation * jax.random.normal(key, dims, jnp.float32)
    if cuts:
        drawn = drawn * level_of(key, dims, cuts, -0.22, 0.18)
    return jnp.clip(drawn, -reach, reach).astype(held_as)


def heavy_noise(stream_key, shape, width, bound, cuts, heavy, held_as=jnp.bfloat16):
    values = width * jax.random.normal(stream_key, shape, jnp.float32)
    if cuts:
        values = values * level_of(stream_key, shape, cuts, -0.22, 0.18)
    return jnp.clip(raised(values, jax.random.fold_in(stream_key, 3), *heavy), -bound, bound).astype(held_as)


def setup_inputs(seed: int = 0) -> dict:
    arg_keys = jax.random.split(jax.random.key(seed), 22)
    return {
        "tokens": bell_draw(arg_keys[0], (TOKENS, D), 1.0, 6.0, ((0, 32),)),
        "cotangent": heavy_noise(arg_keys[1], (TOKENS, D), 1.0, 6.0, ((0, 32),), (0, 1, 32, 2.75)),
        "segments": jax.vmap(lambda own: jnp.searchsorted(jnp.cumsum(uneven(own, DOCS, SEQ, LONGEST, 2)), jnp.arange(SEQ), side="right"))(jax.random.split(arg_keys[2], NSEQ)).reshape((NSEQ, SEQ)).astype(jnp.int32),
        "qkv_weight": bell_draw(arg_keys[3], (D, QKV), D ** -0.5, 0.1875, ((0, 8),), jnp.float32),
        "qkv_moment": bell_draw(arg_keys[4], (D, QKV), (0.111 * (2 * TOKENS) ** 0.5), 128.0, ((0, 8),), jnp.float32),
        "qkv_square": jnp.clip(jnp.exp(math.log(131.072) - 1.3862944 * jax.random.uniform(arg_keys[5], (D, QKV), jnp.float32) ** level_of(arg_keys[5], (D, QKV), ((0, 8),), -0.2, 0.2)), 32.768, 131.072),
        "qkv_bias": bell_draw(arg_keys[6], (QKV,), 0.5, 3.0, ((0, 8),), jnp.float32),
        "bias_moment": bell_draw(arg_keys[7], (QKV,), (0.111 * (2 * TOKENS * D * (QUERY_HEADS // KEY_VALUE_HEADS) // max(4, QUERY_WIDTH // 64)) ** 0.5), 2560.0, ((0, 8),), jnp.float32),
        "bias_square": jnp.clip(jnp.exp(math.log(58720.258) - 1.3862944 * jax.random.uniform(arg_keys[8], (QKV,), jnp.float32) ** level_of(arg_keys[8], (QKV,), ((0, 8),), -0.2, 0.2)), 14680.064, 58720.258),
        "out_weight": bell_draw(arg_keys[9], (QUERY_WIDTH, D), (max(4, QUERY_WIDTH // 64)) ** -0.5, 1.5, ((0, 8),), jnp.float32),
        "out_moment": bell_draw(arg_keys[10], (QUERY_WIDTH, D), (0.111 * (0.015 * TOKENS) ** 0.5), 6.0, ((0, 8),), jnp.float32),
        "out_square": jnp.clip(jnp.exp(math.log(0.98304) - 1.3862944 * jax.random.uniform(arg_keys[11], (QUERY_WIDTH, D), jnp.float32) ** level_of(arg_keys[11], (QUERY_WIDTH, D), ((0, 8),), -0.2, 0.2)), 0.24576, 0.98304),
        "gate_up_weight": bell_draw(arg_keys[12], (D, 2, FF), D ** -0.5, 0.1875, ((0, 8), (2, 4)), jnp.float32),
        "gate_up_moment": bell_draw(arg_keys[13], (D, 2, FF), (0.111 * (0.2 * TOKENS) ** 0.5), 40.0, ((0, 8), (2, 4)), jnp.float32),
        "gate_up_square": jnp.clip(jnp.exp(math.log(13.1072) - 1.3862944 * jax.random.uniform(arg_keys[14], (D, 2, FF), jnp.float32) ** level_of(arg_keys[14], (D, 2, FF), ((0, 8), (2, 4)), -0.2, 0.2)), 3.2768, 13.1072),
        "down_weight": bell_draw(arg_keys[15], (FF, D), (FF // 3) ** -0.5, 0.15625, ((0, 4), (1, 8)), jnp.float32),
        "down_moment": bell_draw(arg_keys[16], (FF, D), (0.111 * (0.36 * TOKENS) ** 0.5), 48.0, ((0, 4), (1, 8)), jnp.float32),
        "down_square": jnp.clip(jnp.exp(math.log(23.59296) - 1.3862944 * jax.random.uniform(arg_keys[17], (FF, D), jnp.float32) ** level_of(arg_keys[17], (FF, D), ((0, 4), (1, 8)), -0.2, 0.2)), 5.89824, 23.59296),
        "norm_gains": jnp.clip(1.0 + 0.1 * jax.random.normal(arg_keys[18], (2, D), jnp.float32), 0.5, 1.5),
        "gains_moment": bell_draw(arg_keys[19], (2, D), (0.111 * (2.5 * TOKENS) ** 0.5), 128.0, ((1, 8),), jnp.float32),
        "gains_square": jnp.clip(jnp.exp(math.log(163.84) - 1.3862944 * jax.random.uniform(arg_keys[20], (2, D), jnp.float32) ** level_of(arg_keys[20], (2, D), ((1, 8),), -0.2, 0.2)), 40.96, 163.84),
    }


@jax.custom_vjp
def lower_precision(v):
    return lax.optimization_barrier(v.astype(jnp.bfloat16)).astype(jnp.float32)

@jax.custom_vjp
def low_back(v):
    return v

def low_keep(v):
    return (lower_precision(v), None)

def low_pass(kept, grad):
    return (grad,)

def back_keep(v):
    return (v, None)

def back_low(kept, grad):
    return (lower_precision(grad),)
lower_precision.defvjp(low_keep, low_pass)
low_back.defvjp(back_keep, back_low)
PRECISE = lax.Precision.HIGHEST
NORM_EPS = 1e-06
ROPE_THETA = 1000000.0
BETA_FIRST = 0.9
BETA_SECOND = 0.999
ADAM_EPS = 1e-08
MASKED = -1e+30

def rms_norm(values, gain):
    factor = lax.rsqrt(lax.optimization_barrier(jnp.mean(values * values, axis=-1, keepdims=True)) + NORM_EPS)
    return values * factor * gain

def apply_rotation(values, cosine_table, sine_lookup):
    half_dim = values.shape[-1] // 2
    first_half = values[..., :half_dim]
    second = values[..., half_dim:]
    cos_b = cosine_table[:, None, :]
    sin_b = sine_lookup[:, None, :]
    return jnp.concatenate([first_half * cos_b - second * sin_b, second * cos_b + first_half * sin_b], axis=-1)

def rotary_tables(segrow):
    document_length = segrow.shape[0]
    before = lax.optimization_barrier(jnp.sum((segrow[None, :] < segrow[:, None]).astype(jnp.int32), axis=1))
    position = jnp.arange(document_length, dtype=jnp.int32) - before
    inverse = ROPE_THETA ** (-(jnp.arange(HEAD_SIZE // 2, dtype=jnp.float32) * 2.0) / HEAD_SIZE)
    angles = position.astype(jnp.float32)[:, None] * inverse[None, :]
    return (jnp.cos(angles), jnp.sin(angles))

def layer_forward(inputs, params, segrow):
    qkv_weight, qkv_bias, out_weight, gate_up_weight, down_weight, norm_gains = params
    document_length = inputs.shape[0]
    group_of_heads = QUERY_HEADS // KEY_VALUE_HEADS
    normed = lower_precision(rms_norm(inputs, norm_gains[0]))
    query_key_value = low_back(jnp.dot(normed, lower_precision(qkv_weight), precision=PRECISE) + qkv_bias)
    cosine_table, sine_lookup = rotary_tables(segrow)
    rotated_queries = query_key_value[:, :QUERY_WIDTH].reshape(document_length, QUERY_HEADS, HEAD_SIZE)
    rotated_keys = query_key_value[:, QUERY_WIDTH:QUERY_WIDTH + KEY_VALUE_HEADS * HEAD_SIZE].reshape(document_length, KEY_VALUE_HEADS, HEAD_SIZE)
    value_matrix = query_key_value[:, QUERY_WIDTH + KEY_VALUE_HEADS * HEAD_SIZE:].reshape(document_length, KEY_VALUE_HEADS, HEAD_SIZE)
    rotated_queries = lower_precision(apply_rotation(rotated_queries, cosine_table, sine_lookup)).reshape(document_length, KEY_VALUE_HEADS, group_of_heads, HEAD_SIZE)
    rotated_keys = lower_precision(apply_rotation(rotated_keys, cosine_table, sine_lookup))
    value_matrix = lower_precision(value_matrix)
    scores = low_back(jnp.einsum('thgd,uhd->hgtu', rotated_queries, rotated_keys, precision=PRECISE) * HEAD_SIZE ** (-0.5))
    token_index = jnp.arange(document_length)
    allowed = (token_index[None, :] <= token_index[:, None]) & (segrow[None, :] == segrow[:, None])
    scores = jnp.where(allowed, scores, MASKED)
    weights = jax.nn.softmax(scores, axis=-1)
    attention_output = jnp.einsum('hgtu,uhd->thgd', lower_precision(weights), value_matrix, precision=PRECISE).reshape(document_length, QUERY_WIDTH)
    attention_output = lower_precision(low_back(attention_output))
    branch = low_back(jnp.dot(attention_output, lower_precision(out_weight), precision=PRECISE))
    hidden = inputs + branch
    normed_two = lower_precision(rms_norm(hidden, norm_gains[1]))
    joined = lower_precision(gate_up_weight).reshape(D, 2 * FF)
    gate_up = low_back(jnp.dot(normed_two, joined, precision=PRECISE)).reshape(document_length, 2, FF)
    active = lower_precision(jax.nn.silu(gate_up[:, 0]) * gate_up[:, 1])
    return hidden + jnp.dot(active, lower_precision(down_weight), precision=PRECISE)

def adam_update(weight, gradient, moment, square, step_rate, decay_rate):
    new_moment = BETA_FIRST * moment + (1.0 - BETA_FIRST) * gradient
    new_square = BETA_SECOND * square + (1.0 - BETA_SECOND) * gradient * gradient
    moment_hat = new_moment / (1.0 - BETA_FIRST ** STEP)
    square_hat = new_square / (1.0 - BETA_SECOND ** STEP)
    updated = weight - step_rate * (moment_hat / (jnp.sqrt(square_hat) + ADAM_EPS) + decay_rate * weight)
    return (gradient, new_moment, new_square, updated)

def reference(tokens, cotangent, segments, qkv_weight, qkv_moment, qkv_square, qkv_bias, bias_moment, bias_square, out_weight, out_moment, out_square, gate_up_weight, gate_up_moment, gate_up_square, down_weight, down_moment, down_square, norm_gains, gains_moment, gains_square):
    params = (qkv_weight, qkv_bias, out_weight, gate_up_weight, down_weight, norm_gains)
    inputs = tokens.astype(jnp.float32).reshape(NSEQ, SEQ, D)
    backs = cotangent.astype(jnp.float32).reshape(NSEQ, SEQ, D)

    def scan_step(grad_total, seq_data):
        seq_rows, seq_back, segrow = seq_data

        def seq_forward(values, weights):
            return layer_forward(values, weights, segrow)
        result, pullback = jax.vjp(seq_forward, seq_rows, params)
        grad_rows, grad_params = pullback(seq_back)
        grad_total = jax.tree.map(lambda left, right: left + right, grad_total, grad_params)
        return (grad_total, (result.astype(jnp.bfloat16), grad_rows.astype(jnp.bfloat16)))
    empty_grads = jax.tree.map(jnp.zeros_like, params)
    grad_total, (results, grad_inputs) = lax.scan(scan_step, empty_grads, (inputs, backs, segments))
    g_qkv, g_bias, g_out, g_gate_up, g_down, g_gains = grad_total
    upd_qkv = adam_update(qkv_weight, g_qkv, qkv_moment, qkv_square, 1.5 * D ** (-0.5), 0.1)
    upd_bias = adam_update(qkv_bias, g_bias, bias_moment, bias_square, 0.3, 0.0)
    upd_out = adam_update(out_weight, g_out, out_moment, out_square, 1.5 * max(4, QUERY_WIDTH // 64) ** (-0.5), 0.1)
    upd_gate_up = adam_update(gate_up_weight, g_gate_up, gate_up_moment, gate_up_square, 1.5 * D ** (-0.5), 0.1)
    upd_down = adam_update(down_weight, g_down, down_moment, down_square, 1.5 * (FF // 3) ** (-0.5), 0.1)
    upd_gains = adam_update(norm_gains, g_gains, gains_moment, gains_square, 0.6, 0.0)
    return (results.reshape(TOKENS, D), grad_inputs.reshape(TOKENS, D), upd_qkv[0], upd_qkv[1], upd_qkv[2], upd_qkv[3], upd_bias[0], upd_bias[1], upd_bias[2], upd_bias[3], upd_out[0], upd_out[1], upd_out[2], upd_out[3], upd_gate_up[0], upd_gate_up[1], upd_gate_up[2], upd_gate_up[3], upd_down[0], upd_down[1], upd_down[2], upd_down[3], upd_gains[0], upd_gains[1], upd_gains[2], upd_gains[3])
```

```python
import jax
import jax.numpy as jnp
from jax import lax
from jax.sharding import PartitionSpec as P

D = 896
QUERY_HEADS = 14
KEY_VALUE_HEADS = 2
HEAD_SIZE = 64
FF = 4864
STEP = 10
QUERY_WIDTH = 896
QKV = 1152


NORM_EPS = 1e-06
ROPE_THETA = 1000000.0
BETA_FIRST = 0.9
BETA_SECOND = 0.999
ADAM_EPS = 1e-08
MASKED = -1e30


def apply_rotation(values, cosine_table, sine_lookup):
    half_dim = values.shape[-1] // 2
    first_half = values[..., :half_dim]
    second = values[..., half_dim:]
    cos_b = cosine_table[:, None, :]
    sin_b = sine_lookup[:, None, :]
    return jnp.concatenate(
        [first_half * cos_b - second * sin_b, second * cos_b + first_half * sin_b], axis=-1
    )


def rotation_backward(values, cosine_table, sine_lookup):
    half_dim = values.shape[-1] // 2
    first_half = values[..., :half_dim]
    second = values[..., half_dim:]
    cos_b = cosine_table[:, None, :]
    sin_b = sine_lookup[:, None, :]
    return jnp.concatenate(
        [first_half * cos_b + second * sin_b, second * cos_b - first_half * sin_b], axis=-1
    )


def contract_rows(left, right):
    return lax.dot_general(
        left, right, (((0,), (0,)), ((), ())), preferred_element_type=jnp.float32
    )


def contract_cols(left, right):
    return lax.dot_general(
        left, right, (((1,), (1,)), ((), ())), preferred_element_type=jnp.float32
    )


def adam_update(weight, gradient, moment, square, step_rate, decay_rate):
    new_moment = BETA_FIRST * moment + (1.0 - BETA_FIRST) * gradient
    new_square = BETA_SECOND * square + (1.0 - BETA_SECOND) * gradient * gradient
    moment_hat = new_moment / (1.0 - BETA_FIRST**STEP)
    square_hat = new_square / (1.0 - BETA_SECOND**STEP)
    updated = weight - step_rate * (
        moment_hat / (jnp.sqrt(square_hat) + ADAM_EPS) + decay_rate * weight
    )
    return (gradient, new_moment, new_square, updated)


def per_device(
    tokens,
    cotangent,
    segments,
    qkv_weight,
    qkv_moment,
    qkv_square,
    qkv_bias,
    bias_moment,
    bias_square,
    out_weight,
    out_moment,
    out_square,
    gate_up_weight,
    gate_up_moment,
    gate_up_square,
    down_weight,
    down_moment,
    down_square,
    norm_gains,
    gains_moment,
    gains_square,
):
    brain_float_cast = jnp.bfloat16
    single_precision = jnp.float32
    token_rows = tokens.shape[0]
    axis_parts = lax.axis_size("mp")
    own_index = lax.axis_index("mp")
    group_of_heads = QUERY_HEADS // KEY_VALUE_HEADS
    width_ff = down_weight.shape[0]
    score_scale = HEAD_SIZE ** (-0.5)
    owned_width = qkv_bias.shape[0]
    gain_width = norm_gains.shape[1]
    owned_rows = qkv_weight.shape[0]
    vectors = jnp.concatenate([qkv_bias, norm_gains[0], norm_gains[1]])
    vectors_high = vectors.astype(brain_float_cast)
    vectors_low = (vectors - vectors_high.astype(single_precision)).astype(brain_float_cast)
    packed = jnp.concatenate([vectors_high, vectors_low])
    packed = jnp.pad(packed, (0, owned_rows * 128 - packed.shape[0])).reshape(owned_rows, 128)
    first_gather = lax.all_gather(
        jnp.concatenate([qkv_weight.astype(brain_float_cast), packed], axis=1),
        "dp",
        axis=0,
        tiled=True,
    )
    w_qkv = first_gather[:, :QKV]
    used = vectors.shape[0]
    unpacked = first_gather[:, QKV:].reshape(-1, owned_rows * 128).astype(single_precision)
    unpacked = unpacked[:, :used] + unpacked[:, used : 2 * used]
    bias_all = unpacked[:, :owned_width].reshape(-1)
    gain_all = (
        unpacked[:, owned_width : owned_width + gain_width].reshape(-1),
        unpacked[:, owned_width + gain_width :].reshape(-1),
    )
    w_out = lax.all_gather(out_weight.astype(brain_float_cast), "dp", axis=0, tiled=True)
    w_ffn = lax.all_gather(
        jnp.concatenate([gate_up_weight[:, 0], gate_up_weight[:, 1], down_weight.T], axis=1).astype(
            brain_float_cast
        ),
        "dp",
        axis=0,
        tiled=True,
    )
    back_all = lax.all_gather(cotangent, "mp", axis=0, tiled=True)
    inputs = tokens.astype(single_precision)
    scale_one = lax.rsqrt(jnp.mean(inputs * inputs, axis=-1, keepdims=True) + NORM_EPS)
    base_one = inputs * scale_one
    normed = (base_one * gain_all[0]).astype(brain_float_cast)
    query_key_value = jnp.dot(normed, w_qkv, preferred_element_type=single_precision) + bias_all
    segrow = segments[0]
    own_seg = lax.dynamic_slice_in_dim(segrow, own_index * token_rows, token_rows)
    before = jnp.sum((segrow[None, :] < own_seg[:, None]).astype(jnp.int32), axis=1)
    query_index = own_index * token_rows + jnp.arange(token_rows, dtype=jnp.int32)
    position = query_index - before
    inverse = ROPE_THETA ** (
        -(jnp.arange(HEAD_SIZE // 2, dtype=single_precision) * 2.0) / HEAD_SIZE
    )
    angles = position.astype(single_precision)[:, None] * inverse[None, :]
    cosine_table = jnp.cos(angles)
    sine_lookup = jnp.sin(angles)
    rotated_queries = apply_rotation(
        query_key_value[:, :QUERY_WIDTH].reshape(token_rows, QUERY_HEADS, HEAD_SIZE),
        cosine_table,
        sine_lookup,
    ).astype(brain_float_cast)
    rotated_keys = apply_rotation(
        query_key_value[:, QUERY_WIDTH : QUERY_WIDTH + KEY_VALUE_HEADS * HEAD_SIZE].reshape(
            token_rows, KEY_VALUE_HEADS, HEAD_SIZE
        ),
        cosine_table,
        sine_lookup,
    )
    rotated_keys = rotated_keys.astype(brain_float_cast).reshape(
        token_rows, KEY_VALUE_HEADS * HEAD_SIZE
    )
    value_matrix = query_key_value[:, QUERY_WIDTH + KEY_VALUE_HEADS * HEAD_SIZE :].astype(
        brain_float_cast
    )
    key_value_all = lax.all_gather(
        jnp.concatenate([rotated_keys, value_matrix], axis=1), "mp", axis=0, tiled=True
    )
    key_all = key_value_all[:, : KEY_VALUE_HEADS * HEAD_SIZE]
    value_all = key_value_all[:, KEY_VALUE_HEADS * HEAD_SIZE :]
    allowed_list = []
    for source in range(axis_parts):
        key_index = source * token_rows + jnp.arange(token_rows, dtype=jnp.int32)
        key_seg = segrow[source * token_rows : (source + 1) * token_rows]
        allowed = (key_index[None, :] <= query_index[:, None]) & (
            key_seg[None, :] == own_seg[:, None]
        )
        allowed_list.append(jnp.repeat(allowed, group_of_heads, axis=0))

    def block_scores(q_block, key_value_head, source):
        key_block = key_all[
            source * token_rows : (source + 1) * token_rows,
            key_value_head * HEAD_SIZE : (key_value_head + 1) * HEAD_SIZE,
        ]
        raw_scores = contract_cols(q_block, key_block) * score_scale
        return jnp.where(allowed_list[source], raw_scores, MASKED)

    query_list = []
    log_totals = []
    head_outputs = []
    for key_value_head in range(KEY_VALUE_HEADS):
        q_block = rotated_queries[
            :, key_value_head * group_of_heads : (key_value_head + 1) * group_of_heads, :
        ].reshape(token_rows * group_of_heads, HEAD_SIZE)
        query_list.append(q_block)
        row_top = jnp.full((token_rows * group_of_heads,), MASKED, single_precision)
        row_total = jnp.zeros((token_rows * group_of_heads,), single_precision)
        for source in range(axis_parts):
            scores = block_scores(q_block, key_value_head, source)
            new_top = jnp.maximum(row_top, jnp.max(scores, axis=-1))
            shifted = jnp.where(allowed_list[source], jnp.exp(scores - new_top[:, None]), 0.0)
            row_total = row_total * jnp.exp(row_top - new_top) + jnp.sum(shifted, axis=-1)
            row_top = new_top
        log_total = row_top + jnp.log(row_total)
        log_totals.append(log_total)
        attended_part = jnp.zeros((token_rows * group_of_heads, HEAD_SIZE), single_precision)
        for source in range(axis_parts):
            scores = block_scores(q_block, key_value_head, source)
            prob_block = jnp.where(
                allowed_list[source], jnp.exp(scores - log_total[:, None]), 0.0
            ).astype(brain_float_cast)
            value_block = value_all[
                source * token_rows : (source + 1) * token_rows,
                key_value_head * HEAD_SIZE : (key_value_head + 1) * HEAD_SIZE,
            ]
            attended_part = attended_part + jnp.dot(
                prob_block, value_block, preferred_element_type=single_precision
            )
        head_outputs.append(attended_part.reshape(token_rows, group_of_heads, HEAD_SIZE))
    attention_output = jnp.stack(head_outputs, axis=1).reshape(token_rows, QUERY_WIDTH)
    attended_low = attention_output.astype(brain_float_cast)
    hidden = inputs + jnp.dot(attended_low, w_out, preferred_element_type=single_precision)
    scale_two = lax.rsqrt(jnp.mean(hidden * hidden, axis=-1, keepdims=True) + NORM_EPS)
    base_two = hidden * scale_two
    normed_two = (base_two * gain_all[1]).astype(brain_float_cast)
    normed_all = lax.all_gather(normed_two, "mp", axis=0, tiled=True)
    joined = w_ffn[:, : 2 * width_ff]
    w_down_t = w_ffn[:, 2 * width_ff :]
    gate_up = jnp.dot(normed_all, joined, preferred_element_type=single_precision)
    gate_pre = gate_up[:, :width_ff]
    up_pre = gate_up[:, width_ff:]
    sig_gate = jax.nn.sigmoid(gate_pre)
    silu_gate = gate_pre * sig_gate
    active = (silu_gate * up_pre).astype(brain_float_cast)
    grad_out = cotangent.astype(single_precision)
    grad_active = jnp.dot(back_all, w_down_t, preferred_element_type=single_precision)
    grad_gate = (grad_active * up_pre * sig_gate * (1.0 + gate_pre * (1.0 - sig_gate))).astype(
        brain_float_cast
    )
    grad_up = (grad_active * silu_gate).astype(brain_float_cast)
    grad_both = jnp.concatenate([grad_gate, grad_up], axis=1)
    normed_partial = contract_cols(grad_both, joined).astype(brain_float_cast)
    grad_normed_two = lax.psum_scatter(
        normed_partial, "mp", scatter_dimension=0, tiled=True
    ).astype(jnp.float32)
    active, grad_both, normed_partial = lax.optimization_barrier(
        (active, grad_both, normed_partial)
    )
    mlp_sum = lax.psum_scatter(
        contract_cols(active, w_down_t).astype(jnp.bfloat16),
        "mp",
        scatter_dimension=0,
        tiled=True,
    ).astype(jnp.float32)
    layer_out = (hidden + mlp_sum).astype(brain_float_cast)
    grad_ffn = jnp.concatenate(
        [
            contract_rows(normed_all, grad_both).astype(brain_float_cast),
            contract_rows(back_all, active).astype(brain_float_cast),
        ],
        axis=1,
    )
    grad_ffn, grad_normed_two = lax.optimization_barrier((grad_ffn, grad_normed_two))
    owned_ffn = lax.psum_scatter(grad_ffn, "dp", scatter_dimension=0, tiled=True).astype(
        single_precision
    )
    grad_gain_two = jnp.sum(grad_normed_two * base_two, axis=0)
    scaled_two = grad_normed_two * gain_all[1]
    grad_hidden = grad_out + scale_two * (
        scaled_two - base_two * jnp.mean(scaled_two * base_two, axis=-1, keepdims=True)
    )
    grad_branch = grad_hidden.astype(brain_float_cast)
    grad_out_w = contract_rows(attended_low, grad_branch)
    attention_output_grad = contract_cols(grad_branch, w_out).astype(brain_float_cast)
    heads_gradient = attention_output_grad.reshape(
        token_rows, KEY_VALUE_HEADS, group_of_heads, HEAD_SIZE
    )
    correction = jnp.sum(
        heads_gradient.astype(single_precision)
        * attention_output.reshape(token_rows, KEY_VALUE_HEADS, group_of_heads, HEAD_SIZE),
        axis=-1,
    )
    grad_query_heads = []
    grad_key_heads = []
    grad_value_heads = []
    for key_value_head in range(KEY_VALUE_HEADS):
        q_block = query_list[key_value_head]
        log_total = log_totals[key_value_head]
        grad_rows_head = heads_gradient[:, key_value_head].reshape(
            token_rows * group_of_heads, HEAD_SIZE
        )
        row_delta = correction[:, key_value_head].reshape(token_rows * group_of_heads)
        grad_query = jnp.zeros((token_rows * group_of_heads, HEAD_SIZE), single_precision)
        key_parts = []
        value_parts = []
        for source in range(axis_parts):
            scores = block_scores(q_block, key_value_head, source)
            prob_block = jnp.where(allowed_list[source], jnp.exp(scores - log_total[:, None]), 0.0)
            key_block = key_all[
                source * token_rows : (source + 1) * token_rows,
                key_value_head * HEAD_SIZE : (key_value_head + 1) * HEAD_SIZE,
            ]
            value_block = value_all[
                source * token_rows : (source + 1) * token_rows,
                key_value_head * HEAD_SIZE : (key_value_head + 1) * HEAD_SIZE,
            ]
            grad_prob = contract_cols(grad_rows_head, value_block)
            grad_score = (prob_block * (grad_prob - row_delta[:, None])).astype(brain_float_cast)
            grad_query = (
                grad_query
                + jnp.dot(grad_score, key_block, preferred_element_type=single_precision)
                * score_scale
            )
            key_parts.append(contract_rows(grad_score, q_block) * score_scale)
            value_parts.append(contract_rows(prob_block.astype(brain_float_cast), grad_rows_head))
        grad_query_heads.append(grad_query.reshape(token_rows, group_of_heads, HEAD_SIZE))
        grad_key_heads.append(jnp.concatenate(key_parts, axis=0))
        grad_value_heads.append(jnp.concatenate(value_parts, axis=0))
    grad_key_all = jnp.concatenate(grad_key_heads, axis=1)
    grad_value_all = jnp.concatenate(grad_value_heads, axis=1)
    key_value_gradient = lax.psum_scatter(
        jnp.concatenate([grad_key_all, grad_value_all], axis=1).astype(jnp.bfloat16),
        "mp",
        scatter_dimension=0,
        tiled=True,
    ).astype(jnp.float32)
    key_gradient = key_value_gradient[:, : KEY_VALUE_HEADS * HEAD_SIZE]
    grad_value = key_value_gradient[:, KEY_VALUE_HEADS * HEAD_SIZE :]
    grad_query_all = jnp.stack(grad_query_heads, axis=1).reshape(token_rows, QUERY_HEADS, HEAD_SIZE)
    grad_query_all = rotation_backward(grad_query_all, cosine_table, sine_lookup).reshape(
        token_rows, QUERY_WIDTH
    )
    key_gradient = rotation_backward(
        key_gradient.reshape(token_rows, KEY_VALUE_HEADS, HEAD_SIZE), cosine_table, sine_lookup
    ).reshape(token_rows, KEY_VALUE_HEADS * HEAD_SIZE)
    grad_qkv = jnp.concatenate([grad_query_all, key_gradient, grad_value], axis=1).astype(
        brain_float_cast
    )
    grad_bias = jnp.sum(grad_qkv.astype(single_precision), axis=0)
    grad_qkv_w = contract_rows(normed, grad_qkv)
    grad_normed = contract_cols(grad_qkv, w_qkv)
    grad_gain_one = jnp.sum(grad_normed * base_one, axis=0)
    scaled_one = grad_normed * gain_all[0]
    grad_inputs = grad_hidden + scale_one * (
        scaled_one - base_one * jnp.mean(scaled_one * base_one, axis=-1, keepdims=True)
    )
    input_grad = grad_inputs.astype(brain_float_cast)
    grad_attention = jnp.concatenate([grad_qkv_w, grad_out_w], axis=1).astype(brain_float_cast)
    grad_attention = lax.psum_scatter(grad_attention, "mp", scatter_dimension=1, tiled=True)
    grad_attention = lax.psum_scatter(grad_attention, "dp", scatter_dimension=0, tiled=True)
    grad_attention = lax.all_gather(grad_attention, "mp", axis=1, tiled=True).astype(
        single_precision
    )
    owned_qkv = grad_attention[:, :QKV]
    owned_out = grad_attention[:, QKV:]
    grad_vectors = jnp.concatenate(
        [
            grad_bias.reshape(-1, owned_width),
            grad_gain_one.reshape(-1, gain_width),
            grad_gain_two.reshape(-1, gain_width),
        ],
        axis=1,
    )
    owned_vectors = lax.dynamic_index_in_dim(
        lax.psum(grad_vectors, ("dp", "mp")), lax.axis_index("dp"), keepdims=False
    )
    owned_bias = owned_vectors[:owned_width]
    owned_gains = owned_vectors[owned_width:].reshape(2, gain_width)
    owned_gate_up = jnp.stack(
        [owned_ffn[:, :width_ff], owned_ffn[:, width_ff : 2 * width_ff]], axis=1
    )
    owned_down = owned_ffn[:, 2 * width_ff :].T
    upd_qkv = adam_update(qkv_weight, owned_qkv, qkv_moment, qkv_square, 1.5 * D ** (-0.5), 0.1)
    upd_bias = adam_update(qkv_bias, owned_bias, bias_moment, bias_square, 0.3, 0.0)
    upd_out = adam_update(
        out_weight,
        owned_out,
        out_moment,
        out_square,
        1.5 * max(4, QUERY_WIDTH // 64) ** (-0.5),
        0.1,
    )
    upd_gate_up = adam_update(
        gate_up_weight, owned_gate_up, gate_up_moment, gate_up_square, 1.5 * D ** (-0.5), 0.1
    )
    upd_down = adam_update(
        down_weight, owned_down, down_moment, down_square, 1.5 * (FF // 3) ** (-0.5), 0.1
    )
    upd_gains = adam_update(norm_gains, owned_gains, gains_moment, gains_square, 0.6, 0.0)
    return (
        layer_out,
        input_grad,
        upd_qkv[0],
        upd_qkv[1],
        upd_qkv[2],
        upd_qkv[3],
        upd_bias[0],
        upd_bias[1],
        upd_bias[2],
        upd_bias[3],
        upd_out[0],
        upd_out[1],
        upd_out[2],
        upd_out[3],
        upd_gate_up[0],
        upd_gate_up[1],
        upd_gate_up[2],
        upd_gate_up[3],
        upd_down[0],
        upd_down[1],
        upd_down[2],
        upd_down[3],
        upd_gains[0],
        upd_gains[1],
        upd_gains[2],
        upd_gains[3],
    )


def solution(mesh):
    placed = (
        P(("dp", "mp"), None),
        P(("dp", "mp"), None),
        P("dp", None),
        P("dp", None),
        P("dp", None),
        P("dp", None),
        P("dp"),
        P("dp"),
        P("dp"),
        P("dp", None),
        P("dp", None),
        P("dp", None),
        P("dp", None, "mp"),
        P("dp", None, "mp"),
        P("dp", None, "mp"),
        P("mp", "dp"),
        P("mp", "dp"),
        P("mp", "dp"),
        P(None, "dp"),
        P(None, "dp"),
        P(None, "dp"),
    )
    return jax.shard_map(
        per_device,
        mesh=mesh,
        in_specs=placed,
        out_specs=(
            P(("dp", "mp"), None),
            P(("dp", "mp"), None),
            P("dp", None),
            P("dp", None),
            P("dp", None),
            P("dp", None),
            P("dp"),
            P("dp"),
            P("dp"),
            P("dp"),
            P("dp", None),
            P("dp", None),
            P("dp", None),
            P("dp", None),
            P("dp", None, "mp"),
            P("dp", None, "mp"),
            P("dp", None, "mp"),
            P("dp", None, "mp"),
            P("mp", "dp"),
            P("mp", "dp"),
            P("mp", "dp"),
            P("mp", "dp"),
            P(None, "dp"),
            P(None, "dp"),
            P(None, "dp"),
            P(None, "dp"),
        ),
        check_vma=False,
    )
```

```python
import jax
import jax.numpy as jnp
from jax import lax
from jax.experimental import pallas as pl
from jax.experimental.pallas import tpu as pltpu
from jax.sharding import PartitionSpec as P

D = 896
QUERY_HEADS = 14
KEY_VALUE_HEADS = 2
HEAD_SIZE = 64
FF = 4864
STEP = 10
QUERY_WIDTH = 896
QKV = 1152


NORM_EPS = 1e-06
ROPE_THETA = 1000000.0
BETA_FIRST = 0.9
BETA_SECOND = 0.999
ADAM_EPS = 1e-08
MASKED = -1e30


def contract_rows(left, right):
    return lax.dot_general(
        left, right, (((0,), (0,)), ((), ())), preferred_element_type=jnp.float32
    )


def contract_cols(left, right):
    return lax.dot_general(
        left, right, (((1,), (1,)), ((), ())), preferred_element_type=jnp.float32
    )


def swap_halves(values):
    lane = lax.broadcasted_iota(jnp.int32, values.shape, 1) % HEAD_SIZE
    return jnp.where(
        lane < HEAD_SIZE // 2,
        pltpu.roll(values, 128 - HEAD_SIZE // 2, 1),
        pltpu.roll(values, HEAD_SIZE // 2, 1),
    )


def attention_forward_kernel(
    place, qkv_ref, cos_ref, sin_ref, start_ref, k_ref, v_ref, q_out, o_out, log_out
):
    rows = qkv_ref.shape[0]
    pair = pl.program_id(0)
    own = place[0]
    x = qkv_ref[...]
    rotated = (x * cos_ref[...] + swap_halves(x) * sin_ref[...]).astype(jnp.bfloat16)
    q_out[...] = rotated
    heads = (rotated[:, :HEAD_SIZE], rotated[:, HEAD_SIZE:])
    starts = start_ref[...]
    query = own * rows + lax.broadcasted_iota(jnp.int32, (rows, rows), 0)

    def step(block, carry):
        at = pl.ds(pl.multiple_of(block * rows, rows), rows)
        key = block * rows + lax.broadcasted_iota(jnp.int32, (rows, rows), 1)
        allowed = (key <= query) & (key >= starts)
        result = []
        for half in range(2):
            top, total, acc = carry[half]
            kv = (pair * 2 + half) // (QUERY_HEADS // KEY_VALUE_HEADS)
            scores = contract_cols(heads[half], k_ref[kv, at, :]) * HEAD_SIZE**-0.5
            scores = jnp.where(allowed, scores, MASKED)
            new_top = jnp.maximum(top, jnp.max(scores, axis=1, keepdims=True))
            weights = jnp.exp(scores - new_top)
            fade = jnp.exp(top - new_top)
            total = total * fade + jnp.sum(weights, axis=1, keepdims=True)
            acc = acc * fade + jnp.dot(
                weights.astype(jnp.bfloat16), v_ref[kv, at, :], preferred_element_type=jnp.float32
            )
            result.append((new_top, total, acc))
        return tuple(result)

    empty = (
        jnp.full((rows, 1), MASKED, jnp.float32),
        jnp.zeros((rows, 1), jnp.float32),
        jnp.zeros((rows, HEAD_SIZE), jnp.float32),
    )
    done = lax.fori_loop(place[1], own + 1, step, (empty, empty))
    o_out[...] = jnp.concatenate([acc / total for _, total, acc in done], axis=1)
    log_out[...] = jnp.concatenate(
        [jnp.broadcast_to(top + jnp.log(total), (rows, HEAD_SIZE)) for top, total, _ in done],
        axis=1,
    )


def attention_backward_kernel(
    place, q_ref, do_ref, o_ref, log_ref, cos_ref, sin_ref, start_ref, k_ref, v_ref, dq_out, dk_out, dv_out
):
    rows = q_ref.shape[0]
    pair = pl.program_id(0)
    own = place[0]

    @pl.when(pair == 0)
    def _():
        dk_out[...] = jnp.zeros_like(dk_out)
        dv_out[...] = jnp.zeros_like(dv_out)

    q = q_ref[...]
    do = do_ref[...]
    log_rows = log_ref[...].T
    products = (do.astype(jnp.float32) * o_ref[...]).T
    starts = start_ref[...]
    query = own * rows + lax.broadcasted_iota(jnp.int32, (rows, rows), 1)

    def step(block, carry):
        at = pl.ds(pl.multiple_of(block * rows, rows), rows)
        key = block * rows + lax.broadcasted_iota(jnp.int32, (rows, rows), 0)
        allowed = (key <= query) & (key >= starts)
        result = []
        for half in range(2):
            lanes = slice(half * HEAD_SIZE, (half + 1) * HEAD_SIZE)
            kv = (pair * 2 + half) // (QUERY_HEADS // KEY_VALUE_HEADS)
            k = k_ref[kv, at, :]
            log_total = log_rows[half * HEAD_SIZE : half * HEAD_SIZE + 1]
            delta = jnp.sum(products[lanes], axis=0, keepdims=True)
            scores = contract_cols(k, q[:, lanes]) * HEAD_SIZE**-0.5
            weights = jnp.exp(jnp.where(allowed, scores - log_total, MASKED))
            dv_out[kv, at, :] += jnp.dot(
                weights.astype(jnp.bfloat16), do[:, lanes], preferred_element_type=jnp.float32
            )
            grad = contract_cols(v_ref[kv, at, :], do[:, lanes])
            grad = (weights * (grad - delta)).astype(jnp.bfloat16)
            dk_out[kv, at, :] += jnp.dot(
                grad, q[:, lanes], preferred_element_type=jnp.float32
            ) * HEAD_SIZE**-0.5
            result.append(carry[half] + contract_rows(grad, k))
        return tuple(result)

    empty = jnp.zeros((rows, HEAD_SIZE), jnp.float32)
    done = lax.fori_loop(place[1], own + 1, step, (empty, empty))
    dq = jnp.concatenate(done, axis=1) * HEAD_SIZE**-0.5
    dq_out[...] = (dq * cos_ref[...] - swap_halves(dq) * sin_ref[...]).astype(jnp.bfloat16)


def column_block(rows):
    return pl.BlockSpec((rows, 128), lambda j, place: (0, j))


def whole_block(array):
    return pl.BlockSpec(array.shape, lambda j, place: (0,) * array.ndim)


def attention_call(kernel, place, blocked, whole, outs, whole_outs, factor):
    rows = blocked[0].shape[0]
    work = QUERY_HEADS * rows * whole[-1].shape[1]
    return pl.pallas_call(
        kernel,
        grid_spec=pltpu.PrefetchScalarGridSpec(
            num_scalar_prefetch=1,
            grid=(QUERY_WIDTH // 128,),
            in_specs=[column_block(rows) for _ in blocked] + [whole_block(a) for a in whole],
            out_specs=[column_block(rows) for _ in outs] + [whole_block(a) for a in whole_outs],
        ),
        out_shape=[jax.ShapeDtypeStruct((rows, QUERY_WIDTH), t) for t in outs] + list(whole_outs),
        compiler_params=pltpu.CompilerParams(vmem_limit_bytes=40 * 2**20),
        cost_estimate=pl.CostEstimate(
            flops=factor * work * 256, bytes_accessed=8 * 2**20, transcendentals=work
        ),
    )(place, *blocked, *whole)


def adam_update(weight, gradient, moment, square, step_rate, decay_rate):
    new_moment = BETA_FIRST * moment + (1.0 - BETA_FIRST) * gradient
    new_square = BETA_SECOND * square + (1.0 - BETA_SECOND) * gradient * gradient
    moment_hat = new_moment / (1.0 - BETA_FIRST**STEP)
    square_hat = new_square / (1.0 - BETA_SECOND**STEP)
    updated = weight - step_rate * (
        moment_hat / (jnp.sqrt(square_hat) + ADAM_EPS) + decay_rate * weight
    )
    return (gradient, new_moment, new_square, updated)


def per_device(
    tokens,
    cotangent,
    segments,
    qkv_weight,
    qkv_moment,
    qkv_square,
    qkv_bias,
    bias_moment,
    bias_square,
    out_weight,
    out_moment,
    out_square,
    gate_up_weight,
    gate_up_moment,
    gate_up_square,
    down_weight,
    down_moment,
    down_square,
    norm_gains,
    gains_moment,
    gains_square,
):
    brain_float_cast = jnp.bfloat16
    single_precision = jnp.float32
    token_rows = tokens.shape[0]
    own_index = lax.axis_index("mp")
    width_ff = down_weight.shape[0]
    owned_width = qkv_bias.shape[0]
    gain_width = norm_gains.shape[1]
    owned_rows = qkv_weight.shape[0]
    vectors = jnp.concatenate([qkv_bias, norm_gains[0], norm_gains[1]])
    vectors_high = vectors.astype(brain_float_cast)
    vectors_low = (vectors - vectors_high.astype(single_precision)).astype(brain_float_cast)
    packed = jnp.concatenate([vectors_high, vectors_low])
    packed = jnp.pad(packed, (0, owned_rows * 128 - packed.shape[0])).reshape(owned_rows, 128)
    first_gather = lax.all_gather(
        jnp.concatenate([qkv_weight.astype(brain_float_cast), packed], axis=1),
        "dp",
        axis=0,
        tiled=True,
    )
    w_qkv = first_gather[:, :QKV]
    used = vectors.shape[0]
    unpacked = first_gather[:, QKV:].reshape(-1, owned_rows * 128).astype(single_precision)
    unpacked = unpacked[:, :used] + unpacked[:, used : 2 * used]
    bias_all = unpacked[:, :owned_width].reshape(-1)
    gain_all = (
        unpacked[:, owned_width : owned_width + gain_width].reshape(-1),
        unpacked[:, owned_width + gain_width :].reshape(-1),
    )
    w_out = lax.all_gather(out_weight.astype(brain_float_cast), "dp", axis=0, tiled=True)
    w_ffn = lax.all_gather(
        jnp.concatenate([gate_up_weight[:, 0], gate_up_weight[:, 1], down_weight.T], axis=1).astype(
            brain_float_cast
        ),
        "dp",
        axis=0,
        tiled=True,
    )
    back_all = lax.all_gather(cotangent, "mp", axis=0, tiled=True)
    inputs = tokens.astype(single_precision)
    scale_one = lax.rsqrt(jnp.mean(inputs * inputs, axis=-1, keepdims=True) + NORM_EPS)
    base_one = inputs * scale_one
    normed = (base_one * gain_all[0]).astype(brain_float_cast)
    query_key_value = jnp.dot(normed, w_qkv, preferred_element_type=single_precision) + bias_all
    segrow = segments[0]
    own_seg = lax.dynamic_slice_in_dim(segrow, own_index * token_rows, token_rows)
    before = jnp.sum((segrow[None, :] < own_seg[:, None]).astype(jnp.int32), axis=1)
    query_index = own_index * token_rows + jnp.arange(token_rows, dtype=jnp.int32)
    position = query_index - before
    inverse = ROPE_THETA ** (
        -(jnp.arange(HEAD_SIZE // 2, dtype=single_precision) * 2.0) / HEAD_SIZE
    )
    angles = position.astype(single_precision)[:, None] * inverse[None, :]
    cosine_table = jnp.cos(angles)
    sine_lookup = jnp.sin(angles)
    cosine_lanes = jnp.tile(cosine_table, (1, 4))
    sine_lanes = jnp.tile(jnp.concatenate([-sine_lookup, sine_lookup], axis=1), (1, 2))

    def swapped(values):
        half = HEAD_SIZE // 2
        return jnp.concatenate(
            [values[:, (p ^ 1) * half : (p ^ 1) * half + half] for p in range(2 * KEY_VALUE_HEADS)],
            axis=1,
        )

    keys = query_key_value[:, QUERY_WIDTH : QUERY_WIDTH + KEY_VALUE_HEADS * HEAD_SIZE]
    rotated_keys = (keys * cosine_lanes + swapped(keys) * sine_lanes).astype(brain_float_cast)
    value_matrix = query_key_value[:, QUERY_WIDTH + KEY_VALUE_HEADS * HEAD_SIZE :].astype(
        brain_float_cast
    )
    key_value_all = lax.all_gather(
        jnp.concatenate([rotated_keys, value_matrix], axis=1), "mp", axis=0, tiled=True
    )
    sequence = key_value_all.shape[0]
    heads_first = key_value_all.reshape(sequence, 2 * KEY_VALUE_HEADS, HEAD_SIZE).swapaxes(0, 1)
    key_heads = heads_first[:KEY_VALUE_HEADS]
    value_heads = heads_first[KEY_VALUE_HEADS:]
    place = jnp.stack([own_index, before[0] // token_rows]).astype(jnp.int32)
    rotated_queries, attention_output, log_totals = attention_call(
        attention_forward_kernel,
        place,
        [query_key_value],
        [cosine_lanes, sine_lanes, before[:, None], key_heads, value_heads],
        [brain_float_cast, single_precision, single_precision],
        [],
        1,
    )
    attention_output, w_ffn, back_all, w_out = lax.optimization_barrier(
        (attention_output, w_ffn, back_all, w_out)
    )
    attended_low = attention_output.astype(brain_float_cast)
    hidden = inputs + jnp.dot(attended_low, w_out, preferred_element_type=single_precision)
    scale_two = lax.rsqrt(jnp.mean(hidden * hidden, axis=-1, keepdims=True) + NORM_EPS)
    base_two = hidden * scale_two
    normed_two = (base_two * gain_all[1]).astype(brain_float_cast)
    normed_all = lax.all_gather(normed_two, "mp", axis=0, tiled=True)
    joined = w_ffn[:, : 2 * width_ff]
    w_down_t = w_ffn[:, 2 * width_ff :]
    gate_up = jnp.dot(normed_all, joined, preferred_element_type=single_precision)
    gate_pre = gate_up[:, :width_ff]
    up_pre = gate_up[:, width_ff:]
    sig_gate = jax.nn.sigmoid(gate_pre)
    silu_gate = gate_pre * sig_gate
    active = (silu_gate * up_pre).astype(brain_float_cast)
    grad_out = cotangent.astype(single_precision)
    grad_active = jnp.dot(back_all, w_down_t, preferred_element_type=single_precision)
    grad_gate = (grad_active * up_pre * sig_gate * (1.0 + gate_pre * (1.0 - sig_gate))).astype(
        brain_float_cast
    )
    grad_up = (grad_active * silu_gate).astype(brain_float_cast)
    grad_both = jnp.concatenate([grad_gate, grad_up], axis=1)
    normed_partial = contract_cols(grad_both, joined).astype(brain_float_cast)
    grad_normed_two = lax.psum_scatter(
        normed_partial, "mp", scatter_dimension=0, tiled=True
    ).astype(jnp.float32)
    active, grad_both, normed_partial = lax.optimization_barrier(
        (active, grad_both, normed_partial)
    )
    mlp_sum = lax.psum_scatter(
        contract_cols(active, w_down_t).astype(jnp.bfloat16),
        "mp",
        scatter_dimension=0,
        tiled=True,
    ).astype(jnp.float32)
    layer_out = (hidden + mlp_sum).astype(brain_float_cast)
    grad_ffn = jnp.concatenate(
        [
            contract_rows(normed_all, grad_both).astype(brain_float_cast),
            contract_rows(back_all, active).astype(brain_float_cast),
        ],
        axis=1,
    )
    grad_ffn, grad_normed_two = lax.optimization_barrier((grad_ffn, grad_normed_two))
    owned_ffn = lax.psum_scatter(grad_ffn, "dp", scatter_dimension=0, tiled=True).astype(
        single_precision
    )
    grad_gain_two = jnp.sum(grad_normed_two * base_two, axis=0)
    scaled_two = grad_normed_two * gain_all[1]
    grad_hidden = grad_out + scale_two * (
        scaled_two - base_two * jnp.mean(scaled_two * base_two, axis=-1, keepdims=True)
    )
    grad_branch = grad_hidden.astype(brain_float_cast)
    grad_out_w = contract_rows(attended_low, grad_branch)
    attention_output_grad = contract_cols(grad_branch, w_out).astype(brain_float_cast)
    attention_shape = jax.ShapeDtypeStruct(key_heads.shape, single_precision)
    grad_query_all, grad_key_heads, grad_value_heads = attention_call(
        attention_backward_kernel,
        place,
        [rotated_queries, attention_output_grad, attention_output, log_totals],
        [cosine_lanes, sine_lanes, before[None, :], key_heads, value_heads],
        [brain_float_cast],
        [attention_shape, attention_shape],
        3,
    )
    grad_key_all = grad_key_heads.swapaxes(0, 1).reshape(sequence, KEY_VALUE_HEADS * HEAD_SIZE)
    grad_value_all = grad_value_heads.swapaxes(0, 1).reshape(
        sequence, KEY_VALUE_HEADS * HEAD_SIZE
    )
    grad_key_all, grad_value_all, owned_ffn = lax.optimization_barrier(
        (grad_key_all, grad_value_all, owned_ffn)
    )
    key_value_gradient = lax.psum_scatter(
        jnp.concatenate([grad_key_all, grad_value_all], axis=1).astype(jnp.bfloat16),
        "mp",
        scatter_dimension=0,
        tiled=True,
    ).astype(jnp.float32)
    key_gradient = key_value_gradient[:, : KEY_VALUE_HEADS * HEAD_SIZE]
    grad_value = key_value_gradient[:, KEY_VALUE_HEADS * HEAD_SIZE :]
    key_gradient = key_gradient * cosine_lanes - swapped(key_gradient) * sine_lanes
    grad_qkv = jnp.concatenate(
        [
            grad_query_all,
            key_gradient.astype(brain_float_cast),
            grad_value.astype(brain_float_cast),
        ],
        axis=1,
    )
    grad_bias = jnp.sum(grad_qkv.astype(single_precision), axis=0)
    grad_qkv_w = contract_rows(normed, grad_qkv)
    grad_normed = contract_cols(grad_qkv, w_qkv)
    grad_gain_one = jnp.sum(grad_normed * base_one, axis=0)
    scaled_one = grad_normed * gain_all[0]
    grad_inputs = grad_hidden + scale_one * (
        scaled_one - base_one * jnp.mean(scaled_one * base_one, axis=-1, keepdims=True)
    )
    input_grad = grad_inputs.astype(brain_float_cast)
    grad_attention = jnp.concatenate([grad_qkv_w, grad_out_w], axis=1).astype(brain_float_cast)
    grad_attention = lax.psum_scatter(grad_attention, "mp", scatter_dimension=1, tiled=True)
    grad_attention = lax.psum_scatter(grad_attention, "dp", scatter_dimension=0, tiled=True)
    grad_attention = lax.all_gather(grad_attention, "mp", axis=1, tiled=True).astype(
        single_precision
    )
    owned_qkv = grad_attention[:, :QKV]
    owned_out = grad_attention[:, QKV:]
    grad_vectors = jnp.concatenate(
        [
            grad_bias.reshape(-1, owned_width),
            grad_gain_one.reshape(-1, gain_width),
            grad_gain_two.reshape(-1, gain_width),
        ],
        axis=1,
    )
    owned_vectors = lax.dynamic_index_in_dim(
        lax.psum(grad_vectors, ("dp", "mp")), lax.axis_index("dp"), keepdims=False
    )
    owned_bias = owned_vectors[:owned_width]
    owned_gains = owned_vectors[owned_width:].reshape(2, gain_width)
    owned_gate_up = jnp.stack(
        [owned_ffn[:, :width_ff], owned_ffn[:, width_ff : 2 * width_ff]], axis=1
    )
    owned_down = owned_ffn[:, 2 * width_ff :].T
    upd_qkv = adam_update(qkv_weight, owned_qkv, qkv_moment, qkv_square, 1.5 * D ** (-0.5), 0.1)
    upd_bias = adam_update(qkv_bias, owned_bias, bias_moment, bias_square, 0.3, 0.0)
    upd_out = adam_update(
        out_weight,
        owned_out,
        out_moment,
        out_square,
        1.5 * max(4, QUERY_WIDTH // 64) ** (-0.5),
        0.1,
    )
    upd_gate_up = adam_update(
        gate_up_weight, owned_gate_up, gate_up_moment, gate_up_square, 1.5 * D ** (-0.5), 0.1
    )
    upd_down = adam_update(
        down_weight, owned_down, down_moment, down_square, 1.5 * (FF // 3) ** (-0.5), 0.1
    )
    upd_gains = adam_update(norm_gains, owned_gains, gains_moment, gains_square, 0.6, 0.0)
    return (
        layer_out,
        input_grad,
        upd_qkv[0],
        upd_qkv[1],
        upd_qkv[2],
        upd_qkv[3],
        upd_bias[0],
        upd_bias[1],
        upd_bias[2],
        upd_bias[3],
        upd_out[0],
        upd_out[1],
        upd_out[2],
        upd_out[3],
        upd_gate_up[0],
        upd_gate_up[1],
        upd_gate_up[2],
        upd_gate_up[3],
        upd_down[0],
        upd_down[1],
        upd_down[2],
        upd_down[3],
        upd_gains[0],
        upd_gains[1],
        upd_gains[2],
        upd_gains[3],
    )


def solution(mesh):
    placed = (
        P(("dp", "mp"), None),
        P(("dp", "mp"), None),
        P("dp", None),
        P("dp", None),
        P("dp", None),
        P("dp", None),
        P("dp"),
        P("dp"),
        P("dp"),
        P("dp", None),
        P("dp", None),
        P("dp", None),
        P("dp", None, "mp"),
        P("dp", None, "mp"),
        P("dp", None, "mp"),
        P("mp", "dp"),
        P("mp", "dp"),
        P("mp", "dp"),
        P(None, "dp"),
        P(None, "dp"),
        P(None, "dp"),
    )
    return jax.shard_map(
        per_device,
        mesh=mesh,
        in_specs=placed,
        out_specs=(
            P(("dp", "mp"), None),
            P(("dp", "mp"), None),
            P("dp", None),
            P("dp", None),
            P("dp", None),
            P("dp", None),
            P("dp"),
            P("dp"),
            P("dp"),
            P("dp"),
            P("dp", None),
            P("dp", None),
            P("dp", None),
            P("dp", None),
            P("dp", None, "mp"),
            P("dp", None, "mp"),
            P("dp", None, "mp"),
            P("dp", None, "mp"),
            P("mp", "dp"),
            P("mp", "dp"),
            P("mp", "dp"),
            P("mp", "dp"),
            P(None, "dp"),
            P(None, "dp"),
            P(None, "dp"),
            P(None, "dp"),
        ),
        check_vma=False,
    )
```
